32 devices in a mesh: gx: 2 (over core), gy: 4 (over z), gz: 4 (over y, x).
Axes of the slice: x: 2, y: 2, z: 4, core: 2. Of those that a mesh axis runs over, the one named last changes fastest.
Arguments:
- gauge_links: float32 [4, 3, 3, 2, 4, 8, 4, 128], P(None, None, None, None, 'gx', 'gy', 'gz'), may hold values from -1 to 1, as said below
- momenta: float32 [4, 3, 3, 2, 4, 8, 4, 128], P(None, None, None, None, 'gx', 'gy', 'gz'), may hold values from -6 to 6, as said below
Outputs:
- new_links: float32 [4, 3, 3, 2, 4, 8, 4, 128], P(None, None, None, None, 'gx', 'gy', 'gz')
- new_momenta: float32 [4, 3, 3, 2, 4, 8, 4, 128], P(None, None, None, None, 'gx', 'gy', 'gz')
The draws below stay inside these ranges and needn't reach their ends.
Inputs may be any that keep to these rules, and one draw needn't show every extreme that they name: `gauge_links`: every link is a unitary 3 x 3 matrix of determinant one. `momenta`: every momentum is an anti-Hermitian 3 x 3 matrix of trace zero.
All inputs are finite; a program needn't handle non-finite values.
Results may differ from the reference program's by a relative error of at most 0.0001.
Values sent between devices are 32-bit elements; how exact they have to be, the bound alone decides.
A program may use at most 64 MiB of HBM per device.

```python
import math
import jax
import jax.numpy as jnp

NT = 128
NX = 4
NY = 8
NZ = 4


def product_drawn(left, right):
    left_real = left[:, :, 0]
    left_imag = left[:, :, 1]
    right_real = right[:, :, 0]
    right_imag = right[:, :, 1]
    real_part = jnp.sum(left_real[:, :, None] * right_real[None] - left_imag[:, :, None] * right_imag[None], axis=1)
    imag_part = jnp.sum(left_real[:, :, None] * right_imag[None] + left_imag[:, :, None] * right_real[None], axis=1)
    return jnp.stack([real_part, imag_part], axis=2)


def assemble(real_rows, imag_rows):
    return jnp.stack([jnp.stack([jnp.stack([real_rows[row_index][column_index], imag_rows[row_index][column_index]]) for column_index in range(3)]) for row_index in range(3)])


def rotation(rotation_angle, height, azimuth, first, second):
    cosine = jnp.cos(rotation_angle)
    sine = jnp.sin(rotation_angle)
    lateral = jnp.sqrt(1.0 - height * height)
    comp_one = sine * lateral * jnp.cos(azimuth)
    comp_two = sine * lateral * jnp.sin(azimuth)
    comp_three = sine * height
    zeros = jnp.zeros_like(cosine)
    ones = jnp.ones_like(cosine)
    third = 3 - first - second
    real_rows = [[zeros, zeros, zeros] for unused_row in range(3)]
    imag_rows = [[zeros, zeros, zeros] for unused_row in range(3)]
    real_rows[first][first] = cosine
    imag_rows[first][first] = comp_three
    real_rows[first][second] = comp_two
    imag_rows[first][second] = comp_one
    real_rows[second][first] = -comp_two
    imag_rows[second][first] = comp_one
    real_rows[second][second] = cosine
    imag_rows[second][second] = -comp_three
    real_rows[third][third] = ones
    return assemble(real_rows, imag_rows)


def draw_gauge_links(key, part):
    extent = (4, NX, NY, NZ, NT)
    keys = jax.random.split(key, 9)
    highest = math.pi
    pairs = ((0, 1), (1, 2), (0, 2))
    running = None
    for number in range(3):
        rotation_angle = jax.random.uniform(keys[3 * number], extent, jnp.float32, 0.0, highest)
        height = jax.random.uniform(keys[3 * number + 1], extent, jnp.float32, -1.0, 1.0)
        azimuth = jax.random.uniform(keys[3 * number + 2], extent, jnp.float32, -math.pi, math.pi)
        factor = rotation(rotation_angle, height, azimuth, pairs[number][0], pairs[number][1])
        running = factor if number == 0 else product_drawn(running, factor)
    return jnp.moveaxis(running, 3, 0).astype(jnp.float32)


def draw_momenta(key, part):
    extent = (8, 4, NX, NY, NZ, NT)
    values = jax.random.truncated_normal(key, -3.0, 3.0, extent, jnp.float32)
    zeros = jnp.zeros_like(values[0])
    diag_one = values[0]
    diag_two = values[1]
    diag_three = -diag_one - diag_two
    real_rows = [[zeros, -values[5], -values[6]], [values[5], zeros, -values[7]], [values[6], values[7], zeros]]
    imag_rows = [[diag_one, values[2], values[3]], [values[2], diag_two, values[4]], [values[3], values[4], diag_three]]
    matrix = assemble(real_rows, imag_rows)
    return jnp.moveaxis(matrix, 3, 0).astype(jnp.float32)


def setup_inputs(seed: int = 0) -> dict:
    key_of = jax.random.split(jax.random.key(seed), 3)
    gauge_links = draw_gauge_links(jax.random.fold_in(key_of[2], 71), 0)
    momenta = draw_momenta(jax.random.fold_in(key_of[2], 71), 0)
    return {"gauge_links": gauge_links, "momenta": momenta}


BETA = 5.7
STEP = 0.25


def product(left, right):
    left_real = left[:, :, 0]
    left_imag = left[:, :, 1]
    right_real = right[:, :, 0]
    right_imag = right[:, :, 1]
    real_part = jnp.sum(left_real[:, :, None] * right_real[None] - left_imag[:, :, None] * right_imag[None], axis=1)
    imag_part = jnp.sum(left_real[:, :, None] * right_imag[None] + left_imag[:, :, None] * right_real[None], axis=1)
    return jnp.stack([real_part, imag_part], axis=2)


def dagger(matrix):
    return jnp.stack([jnp.swapaxes(matrix[:, :, 0], 0, 1), -jnp.swapaxes(matrix[:, :, 1], 0, 1)], axis=2)


def add_identity(matrix):
    identity = jnp.eye(3, dtype=jnp.float32).reshape((3, 3) + (1,) * (matrix.ndim - 3))
    return jnp.stack([matrix[:, :, 0] + identity, matrix[:, :, 1]], axis=2)


def exponent(generator):
    series = add_identity(generator / 4.0)
    series = add_identity(product(generator, series) / 3.0)
    series = add_identity(product(generator, series) / 2.0)
    return add_identity(product(generator, series))


def project(omega):
    real_part = 0.5 * (omega[:, :, 0] - jnp.swapaxes(omega[:, :, 0], 0, 1))
    imag_part = 0.5 * (omega[:, :, 1] + jnp.swapaxes(omega[:, :, 1], 0, 1))
    trace = (omega[0, 0, 1] + omega[1, 1, 1] + omega[2, 2, 1]) / 3.0
    identity = jnp.eye(3, dtype=jnp.float32).reshape((3, 3) + (1,) * trace.ndim)
    imag_part = imag_part - identity * trace
    return jnp.stack([real_part, imag_part], axis=2)


def move(matrix, direction, amount):
    return jnp.roll(matrix, -amount, axis=3 + direction)


def forces(field):
    result = []
    for along in range(4):
        running = jnp.zeros_like(field[along])
        for across in range(4):
            if across == along:
                continue
            upper = product(product(move(field[across], along, 1), dagger(move(field[along], across, 1))), dagger(field[across]))
            lower_site = product(product(dagger(move(field[across], along, 1)), dagger(field[along])), field[across])
            lower = move(lower_site, across, -1)
            running = running + upper + lower
        omega = product(field[along], running)
        result.append((BETA / 3.0) * project(omega))
    return result


def reference(gauge_links, momenta):
    field = [gauge_links[direction] for direction in range(4)]
    moment = [momenta[direction] for direction in range(4)]
    kick = forces(field)
    moment = [moment[direction] - (0.5 * STEP) * kick[direction] for direction in range(4)]
    for repeat in range(2):
        field = [product(exponent(STEP * moment[direction]), field[direction]) for direction in range(4)]
        kick = forces(field)
        factor = STEP if repeat == 0 else 0.5 * STEP
        moment = [moment[direction] - factor * kick[direction] for direction in range(4)]
    return jnp.stack(field), jnp.stack(moment)
```

```python
import jax
import jax.numpy as jnp
from jax import lax
from jax.experimental import pallas as pl
from jax.experimental.pallas import tpu as pltpu
from jax.sharding import PartitionSpec as P

BETA = 5.7
STEP = 0.25
AXES = ("gx", "gy", "gz")
MESH = pl.DeviceIdType.MESH

MOMENT_PLANES = (2, 4, 10, 3, 5, 11, 1, 9)


def matrix(planes):
    return [
        [(planes[(row * 3 + column) * 2], planes[(row * 3 + column) * 2 + 1]) for column in range(3)]
        for row in range(3)
    ]


def dagger(value):
    return ("dagger", value)


def entry(value, row, column):
    if isinstance(value, tuple):
        real, imag = value[1][column][row]
        return real, imag, True
    real, imag = value[row][column]
    return real, imag, False


def product(left, right):
    result = []
    for row in range(3):
        line = []
        for column in range(3):
            real = imag = None
            for inner in range(3):
                lr, li, lc = entry(left, row, inner)
                rr, ri, rc = entry(right, inner, column)
                rr_part = lr * rr
                ii_part = li * ri
                ri_part = lr * ri
                ir_part = li * rr
                first = rr_part - ii_part if lc == rc else rr_part + ii_part
                if real is None:
                    real = first
                    if rc and lc:
                        imag = -(ri_part + ir_part)
                    elif rc:
                        imag = ir_part - ri_part
                    elif lc:
                        imag = ri_part - ir_part
                    else:
                        imag = ri_part + ir_part
                else:
                    real = real + first
                    imag = imag - ri_part if rc else imag + ri_part
                    imag = imag - ir_part if lc else imag + ir_part
            line.append((real, imag))
        result.append(line)
    return result


def project(omega):
    third = (omega[0][0][1] + omega[1][1][1] + omega[2][2][1]) * (1.0 / 3.0)
    return [
        0.5 * (omega[0][1][0] - omega[1][0][0]),
        0.5 * (omega[0][2][0] - omega[2][0][0]),
        0.5 * (omega[1][2][0] - omega[2][1][0]),
        0.5 * (omega[0][1][1] + omega[1][0][1]),
        0.5 * (omega[0][2][1] + omega[2][0][1]),
        0.5 * (omega[1][2][1] + omega[2][1][1]),
        omega[0][0][1] - third,
        omega[1][1][1] - third,
    ]


def exponent(planes):
    r01, r02, r12, s01, s02, s12, s00, s11 = [STEP * plane for plane in planes]
    s22 = -(s00 + s11)
    n01 = s01 * s01 + r01 * r01
    n02 = s02 * s02 + r02 * r02
    n12 = s12 * s12 + r12 * r12
    q00 = s00 * s00 + n01 + n02
    q11 = s11 * s11 + n01 + n12
    q22 = s22 * s22 + n02 + n12
    a_re = s01 * s12 - r01 * r12
    a_im = -(s01 * r12 + r01 * s12)
    q01_re = s02 * s12 + r02 * r12 - s01 * s22
    q01_im = s02 * r12 - r02 * s12 + r01 * s22
    q02_re = a_re - s02 * s11
    q02_im = a_im + r02 * s11
    q12_re = s01 * s02 + r01 * r02 - s12 * s00
    q12_im = r01 * s02 - s01 * r02 + r12 * s00
    half_trace = 0.5 * (q00 + q11 + q22)
    determinant = (
        s00 * (s11 * s22 - n12) - s11 * n02 - s22 * n01 + 2.0 * (a_re * s02 - a_im * r02)
    )
    alpha_im = determinant * (-1.0 / 6.0)
    beta_re = determinant * (1.0 / 24.0)
    beta_im = 1.0 - half_trace * (1.0 / 6.0)
    gamma = half_trace * (1.0 / 24.0) - 0.5

    def diagonal(s, q):
        return 1.0 + beta_re * s + gamma * q, alpha_im + beta_im * s

    def pair(s, r, q_re, q_im):
        even_re = beta_re * s + gamma * q_re
        even_im = gamma * q_im - beta_re * r
        odd_re = beta_im * r
        odd_im = beta_im * s
        upper = (even_re + odd_re, even_im + odd_im)
        lower = (even_re - odd_re, odd_im - even_im)
        return upper, lower

    e01, e10 = pair(s01, r01, q01_re, q01_im)
    e02, e20 = pair(s02, r02, q02_re, q02_im)
    e12, e21 = pair(s12, r12, q12_re, q12_im)
    return [
        [diagonal(s00, q00), e01, e02],
        [e10, diagonal(s11, q11), e12],
        [e20, e21, diagonal(s22, q22)],
    ]


def advance(moment_ref, field_ref):
    step = exponent([moment_ref[plane] for plane in range(8)])
    moved = product(step, matrix([field_ref[plane] for plane in range(18)]))
    for row in range(3):
        for column in range(3):
            for part in range(2):
                field_ref[(row * 3 + column) * 2 + part] = moved[row][column][part]


def kernel(
    links_in, moment_in, links_out, moment_out,
    field, halo, moment, moment_halo, kicks, kicks_in, local, operands, results,
    field_send, field_recv, moment_send, moment_recv, kick_send, kick_recv,
):
    coords = [lax.axis_index(axis) for axis in AXES]
    counts = [lax.axis_size(axis) for axis in AXES]

    def neighbour(axis, steps):
        place = list(coords)
        place[axis] = lax.rem(coords[axis] + (steps + counts[axis]), counts[axis])
        return tuple(place)

    barrier = pltpu.get_barrier_semaphore()
    for axis in range(3):
        for steps in (-1, 1):
            pl.semaphore_signal(barrier, inc=1, device_id=neighbour(axis, steps), device_id_type=MESH)

    for half in range(2):
        field[half] = jnp.concatenate([links_in[2 * half], links_in[2 * half + 1]], axis=1)
        for plane, source in enumerate(MOMENT_PLANES):
            moment[half, plane] = jnp.concatenate(
                [moment_in[2 * half, source], moment_in[2 * half + 1, source]], axis=0
            )
    pl.semaphore_wait(barrier, 6)

    def field_copy(axis):
        return pltpu.make_async_remote_copy(
            src_ref=field, dst_ref=halo.at[axis],
            send_sem=field_send.at[axis], recv_sem=field_recv.at[axis],
            device_id=neighbour(axis, -1), device_id_type=MESH,
        )

    def moment_copy(repeat, axis):
        return pltpu.make_async_remote_copy(
            src_ref=moment, dst_ref=moment_halo.at[repeat, axis],
            send_sem=moment_send.at[repeat, axis], recv_sem=moment_recv.at[repeat, axis],
            device_id=neighbour(axis, -1), device_id_type=MESH,
        )

    def kick_copy(repeat, axis):
        return pltpu.make_async_remote_copy(
            src_ref=kicks.at[axis], dst_ref=kicks_in.at[repeat, axis],
            send_sem=kick_send.at[repeat, axis], recv_sem=kick_recv.at[repeat, axis],
            device_id=neighbour(axis, 1), device_id_type=MESH,
        )

    for axis in (2, 1, 0):
        field_copy(axis).start()

    row = lax.broadcasted_iota(jnp.int32, (1, 8, 128), 1)
    top = row < 4
    near_x = lax.rem(row, 4) < 2
    near_y = lax.rem(row, 2) < 1

    def select(mask, first, second):
        return jnp.where(jnp.broadcast_to(mask, first.shape), first, second)

    def flip(value):
        return pltpu.roll(value, 4, 1)

    def swap_x(value):
        return select(near_x, pltpu.roll(value, 6, 1), pltpu.roll(value, 2, 1))

    def swap_y(value):
        return select(near_y, pltpu.roll(value, 7, 1), pltpu.roll(value, 1, 1))

    def ahead_x(half):
        return swap_x(select(near_x, halo[0, half], field[half]))

    def ahead_y(half):
        return swap_y(select(near_y, halo[1, half], field[half]))

    def ahead_t(half):
        return pltpu.roll(field[half], 127, 2)

    def gather_operands():
        operands[0, 0] = field[0]
        operands[1, 0] = field[0]
        operands[0, 3] = field[1]
        operands[1, 3] = flip(field[1])
        operands[2, 0] = select(top, field[0], flip(field[1]))
        operands[2, 3] = select(top, flip(field[0]), field[1])
        x_one = ahead_x(1)
        y_one = ahead_y(1)
        operands[0, 1] = select(top, x_one, y_one)
        operands[1, 1] = flip(select(top, y_one, x_one))
        operands[2, 1] = select(top, flip(ahead_x(0)), halo[2, 1])
        t_zero = ahead_t(0)
        operands[0, 2] = select(top, halo[2, 0], t_zero)
        operands[1, 2] = select(top, t_zero, halo[2, 0])
        operands[2, 2] = select(top, ahead_y(0), flip(ahead_t(1)))

    def group(number, carry):
        def load(which):
            return matrix([operands[number, which, plane] for plane in range(18)])

        def store(which, value):
            for plane, part in enumerate(project(value)):
                results[number, which, plane] = part

        here, along, across, side = load(0), load(1), load(2), load(3)
        one = product(here, along)
        two = product(side, across)
        store(0, product(one, dagger(two)))
        store(1, product(across, product(dagger(one), side)))
        store(2, product(along, product(dagger(two), here)))
        return carry

    def round_of(repeat, carry):
        gather_operands()
        lax.fori_loop(0, 3, group, 0)

        zero = jnp.zeros((8, 8, 128), jnp.float32)
        nu_a, nu_b, nu_c = results[0, 2], results[1, 2], results[2, 2]
        mu_a, mu_b, mu_c = results[0, 1], results[1, 1], results[2, 1]
        kicks[2, 0] = select(top, mu_a, mu_b)
        kicks[2, 1] = select(top, zero, nu_c)
        kick_copy(repeat, 2).start()
        nu_b = flip(nu_b)
        kicks[1, 0] = select(top, mu_c, zero)
        kicks[1, 1] = select(top, nu_b, nu_a)
        kick_copy(repeat, 1).start()
        kicks[0, 0] = select(top, zero, flip(nu_c))
        kicks[0, 1] = select(top, nu_a, nu_b)
        kick_copy(repeat, 0).start()
        p_a, p_b, p_c = results[0, 0], results[1, 0], results[2, 0]
        q_c = flip(p_c)
        local[0] = (
            p_a + p_b + select(top, p_c, -q_c) + pltpu.roll(select(top, mu_b, mu_a), 1, 2)
        )
        local[1] = (
            select(top, q_c, -p_c) - p_a - flip(p_b)
            + pltpu.roll(select(top, flip(mu_c), zero), 1, 2)
        )
        kick_copy(repeat, 0).wait()
        for half in range(2):
            local[half] += swap_x(select(near_x, kicks[0, half], kicks_in[repeat, 0, half]))
        kick_copy(repeat, 1).wait()
        for half in range(2):
            local[half] += swap_y(select(near_y, kicks[1, half], kicks_in[repeat, 1, half]))
        kick_copy(repeat, 2).wait()
        factor = jnp.where(repeat == 1, STEP * BETA / 3.0, 0.5 * STEP * BETA / 3.0)
        for half in range(2):
            moment[half] = moment[half] - factor * (local[half] + kicks_in[repeat, 2, half])

        @pl.when(repeat < 2)
        def _():
            for axis in (2, 1, 0):
                moment_copy(repeat, axis).start()

            def own(half, carry):
                advance(moment.at[half], field.at[half])
                return carry

            lax.fori_loop(0, 2, own, 0)

            def arrived(axis, carry):
                moment_copy(repeat, axis).wait()

                def ahead(half, carry):
                    advance(moment_halo.at[repeat, axis, half], halo.at[axis, half])
                    return carry

                return lax.fori_loop(0, 2, ahead, carry)

            for axis in range(3):
                arrived(axis, 0)

        return carry

    for axis in range(3):
        field_copy(axis).wait()
    lax.fori_loop(0, 3, round_of, 0)

    for half in range(2):
        for place in range(2):
            rows = slice(4 * place, 4 * place + 4)
            links_out[2 * half + place] = field[half, :, rows, :]
        r01, r02, r12, s01, s02, s12, s00, s11 = [moment[half, plane] for plane in range(8)]
        zero = jnp.zeros_like(r01)
        planes = [
            zero, s00, r01, s01, r02, s02,
            -r01, s01, zero, s11, r12, s12,
            -r02, s02, -r12, s12, zero, -(s00 + s11),
        ]
        for plane, value in enumerate(planes):
            moment_out[2 * half, plane] = value[0:4]
            moment_out[2 * half + 1, plane] = value[4:8]


def body(gauge_links, momenta):
    shape = gauge_links.shape
    assert shape == (4, 3, 3, 2, 2, 2, 1, 128)
    whole = jax.ShapeDtypeStruct((4, 18, 4, 128), jnp.float32)
    vmem = pl.BlockSpec(memory_space=pltpu.VMEM)
    links, moment = pl.pallas_call(
        kernel,
        out_shape=(whole, whole),
        in_specs=[vmem, vmem],
        out_specs=(vmem, vmem),
        scratch_shapes=[
            pltpu.VMEM((2, 18, 8, 128), jnp.float32),
            pltpu.VMEM((3, 2, 18, 8, 128), jnp.float32),
            pltpu.VMEM((2, 8, 8, 128), jnp.float32),
            pltpu.VMEM((2, 3, 2, 8, 8, 128), jnp.float32),
            pltpu.VMEM((3, 2, 8, 8, 128), jnp.float32),
            pltpu.VMEM((3, 3, 2, 8, 8, 128), jnp.float32),
            pltpu.VMEM((2, 8, 8, 128), jnp.float32),
            pltpu.VMEM((3, 4, 18, 8, 128), jnp.float32),
            pltpu.VMEM((3, 3, 8, 8, 128), jnp.float32),
            pltpu.SemaphoreType.DMA((3,)),
            pltpu.SemaphoreType.DMA((3,)),
            pltpu.SemaphoreType.DMA((2, 3)),
            pltpu.SemaphoreType.DMA((2, 3)),
            pltpu.SemaphoreType.DMA((3, 3)),
            pltpu.SemaphoreType.DMA((3, 3)),
        ],
        compiler_params=pltpu.CompilerParams(
            collective_id=0, has_side_effects=True, vmem_limit_bytes=16 * 1024 * 1024
        ),
    )(gauge_links.reshape(4, 18, 4, 128), momenta.reshape(4, 18, 4, 128))
    return links.reshape(shape), moment.reshape(shape)


def solution(mesh):
    spec = P(None, None, None, None, "gx", "gy", "gz", None)
    return jax.shard_map(
        body, mesh=mesh, in_specs=(spec, spec), out_specs=(spec, spec), check_vma=False
    )
```

```python
import jax
import jax.numpy as jnp
from jax import lax
from jax.experimental import pallas as pl
from jax.experimental.pallas import tpu as pltpu
from jax.sharding import PartitionSpec as P

BETA = 5.7
STEP = 0.25
AXES = ("gx", "gy", "gz")
MESH = pl.DeviceIdType.MESH
EDGES = ((1, 2), (2, 1))

MOMENT_PLANES = (2, 4, 10, 3, 5, 11, 1, 9)


def matrix(planes):
    return [
        [(planes[(row * 3 + column) * 2], planes[(row * 3 + column) * 2 + 1]) for column in range(3)]
        for row in range(3)
    ]


def dagger(value):
    return ("dagger", value)


def entry(value, row, column):
    if isinstance(value, tuple):
        real, imag = value[1][column][row]
        return real, imag, True
    real, imag = value[row][column]
    return real, imag, False


def product(left, right):
    result = []
    for row in range(3):
        line = []
        for column in range(3):
            real = imag = None
            for inner in range(3):
                lr, li, lc = entry(left, row, inner)
                rr, ri, rc = entry(right, inner, column)
                rr_part = lr * rr
                ii_part = li * ri
                ri_part = lr * ri
                ir_part = li * rr
                first = rr_part - ii_part if lc == rc else rr_part + ii_part
                if real is None:
                    real = first
                    if rc and lc:
                        imag = -(ri_part + ir_part)
                    elif rc:
                        imag = ir_part - ri_part
                    elif lc:
                        imag = ri_part - ir_part
                    else:
                        imag = ri_part + ir_part
                else:
                    real = real + first
                    imag = imag - ri_part if rc else imag + ri_part
                    imag = imag - ir_part if lc else imag + ir_part
            line.append((real, imag))
        result.append(line)
    return result


def project(omega):
    third = (omega[0][0][1] + omega[1][1][1] + omega[2][2][1]) * (1.0 / 3.0)
    return [
        0.5 * (omega[0][1][0] - omega[1][0][0]),
        0.5 * (omega[0][2][0] - omega[2][0][0]),
        0.5 * (omega[1][2][0] - omega[2][1][0]),
        0.5 * (omega[0][1][1] + omega[1][0][1]),
        0.5 * (omega[0][2][1] + omega[2][0][1]),
        0.5 * (omega[1][2][1] + omega[2][1][1]),
        omega[0][0][1] - third,
        omega[1][1][1] - third,
    ]


def exponent(planes):
    r01, r02, r12, s01, s02, s12, s00, s11 = [STEP * plane for plane in planes]
    s22 = -(s00 + s11)
    n01 = s01 * s01 + r01 * r01
    n02 = s02 * s02 + r02 * r02
    n12 = s12 * s12 + r12 * r12
    q00 = s00 * s00 + n01 + n02
    q11 = s11 * s11 + n01 + n12
    q22 = s22 * s22 + n02 + n12
    a_re = s01 * s12 - r01 * r12
    a_im = -(s01 * r12 + r01 * s12)
    q01_re = s02 * s12 + r02 * r12 - s01 * s22
    q01_im = s02 * r12 - r02 * s12 + r01 * s22
    q02_re = a_re - s02 * s11
    q02_im = a_im + r02 * s11
    q12_re = s01 * s02 + r01 * r02 - s12 * s00
    q12_im = r01 * s02 - s01 * r02 + r12 * s00
    half_trace = 0.5 * (q00 + q11 + q22)
    determinant = (
        s00 * (s11 * s22 - n12) - s11 * n02 - s22 * n01 + 2.0 * (a_re * s02 - a_im * r02)
    )
    alpha_im = determinant * (-1.0 / 6.0)
    beta_re = determinant * (1.0 / 24.0)
    beta_im = 1.0 - half_trace * (1.0 / 6.0)
    gamma = half_trace * (1.0 / 24.0) - 0.5

    def diagonal(s, q):
        return 1.0 + beta_re * s + gamma * q, alpha_im + beta_im * s

    def pair(s, r, q_re, q_im):
        even_re = beta_re * s + gamma * q_re
        even_im = gamma * q_im - beta_re * r
        odd_re = beta_im * r
        odd_im = beta_im * s
        upper = (even_re + odd_re, even_im + odd_im)
        lower = (even_re - odd_re, odd_im - even_im)
        return upper, lower

    e01, e10 = pair(s01, r01, q01_re, q01_im)
    e02, e20 = pair(s02, r02, q02_re, q02_im)
    e12, e21 = pair(s12, r12, q12_re, q12_im)
    return [
        [diagonal(s00, q00), e01, e02],
        [e10, diagonal(s11, q11), e12],
        [e20, e21, diagonal(s22, q22)],
    ]


def advance(moment_ref, field_ref):
    step = exponent([moment_ref[plane] for plane in range(8)])
    moved = product(step, matrix([field_ref[plane] for plane in range(18)]))
    for row in range(3):
        for column in range(3):
            for part in range(2):
                field_ref[(row * 3 + column) * 2 + part] = moved[row][column][part]


def kernel(
    links_in, moment_in, links_out, moment_out,
    field, halo, moment, partial, moment_halo, kicks, kicks_in, edge_out, edge_in, operands, results,
    field_send, field_recv, moment_send, moment_recv, kick_send, kick_recv, edge_send, edge_recv,
):
    coords = [lax.axis_index(axis) for axis in AXES]
    counts = [lax.axis_size(axis) for axis in AXES]

    def displaced(*moves):
        place = list(coords)
        for axis, steps in moves:
            place[axis] = lax.rem(coords[axis] + (steps + counts[axis]), counts[axis])
        return tuple(place)

    def neighbour(axis, steps):
        return displaced((axis, steps))

    barrier = pltpu.get_barrier_semaphore()
    for axis in range(3):
        for steps in (-1, 1):
            pl.semaphore_signal(barrier, inc=1, device_id=neighbour(axis, steps), device_id_type=MESH)

    for behind, along in EDGES:
        pl.semaphore_signal(
            barrier, inc=1, device_id=displaced((along, 1), (behind, -1)), device_id_type=MESH
        )

    for half in range(2):
        field[half] = jnp.concatenate([links_in[2 * half], links_in[2 * half + 1]], axis=1)
        for plane, source in enumerate(MOMENT_PLANES):
            moment[half, plane] = jnp.concatenate(
                [moment_in[2 * half, source], moment_in[2 * half + 1, source]], axis=0
            )
    pl.semaphore_wait(barrier, 8)

    def field_copy(axis):
        return pltpu.make_async_remote_copy(
            src_ref=field.at[:, pl.ds(0, 12)], dst_ref=halo.at[axis, :, pl.ds(0, 12)],
            send_sem=field_send.at[axis], recv_sem=field_recv.at[axis],
            device_id=neighbour(axis, -1), device_id_type=MESH,
        )

    def moment_copy(repeat, axis):
        return pltpu.make_async_remote_copy(
            src_ref=moment if axis == 0 else partial, dst_ref=moment_halo.at[repeat, axis],
            send_sem=moment_send.at[repeat, axis], recv_sem=moment_recv.at[repeat, axis],
            device_id=neighbour(axis, -1), device_id_type=MESH,
        )

    def kick_copy(repeat, axis):
        return pltpu.make_async_remote_copy(
            src_ref=kicks.at[axis], dst_ref=kicks_in.at[repeat, axis],
            send_sem=kick_send.at[repeat, axis], recv_sem=kick_recv.at[repeat, axis],
            device_id=neighbour(axis, 1), device_id_type=MESH,
        )

    def edge_copy(repeat, number):
        behind, along = EDGES[number]
        return pltpu.make_async_remote_copy(
            src_ref=edge_out.at[number], dst_ref=edge_in.at[repeat, number],
            send_sem=edge_send.at[repeat, number], recv_sem=edge_recv.at[repeat, number],
            device_id=displaced((along, 1), (behind, -1)), device_id_type=MESH,
        )

    for axis in (2, 1, 0):
        field_copy(axis).start()

    row = lax.broadcasted_iota(jnp.int32, (1, 8, 128), 1)
    top = row < 4
    near_x = lax.rem(row, 4) < 2
    near_y = lax.rem(row, 2) < 1

    def select(mask, first, second):
        return jnp.where(jnp.broadcast_to(mask, first.shape), first, second)

    def flip(value):
        return pltpu.roll(value, 4, 1)

    def swap_x(value):
        return select(near_x, pltpu.roll(value, 6, 1), pltpu.roll(value, 2, 1))

    def swap_y(value):
        return select(near_y, pltpu.roll(value, 7, 1), pltpu.roll(value, 1, 1))

    def ahead_x(half):
        return swap_x(select(near_x, halo[0, half], field[half]))

    def ahead_y(half):
        return swap_y(select(near_y, halo[1, half], field[half]))

    def ahead_t(half):
        return pltpu.roll(field[half], 127, 2)

    def gather_operands():
        operands[0, 0] = field[0]
        operands[1, 0] = field[0]
        operands[0, 3] = field[1]
        operands[1, 3] = flip(field[1])
        operands[2, 0] = select(top, field[0], flip(field[1]))
        operands[2, 3] = select(top, flip(field[0]), field[1])
        x_one = ahead_x(1)
        y_one = ahead_y(1)
        operands[0, 1] = select(top, x_one, y_one)
        operands[1, 1] = flip(select(top, y_one, x_one))
        operands[2, 1] = select(top, flip(ahead_x(0)), halo[2, 1])
        t_zero = ahead_t(0)
        operands[0, 2] = select(top, halo[2, 0], t_zero)
        operands[1, 2] = select(top, t_zero, halo[2, 0])
        operands[2, 2] = select(top, ahead_y(0), flip(ahead_t(1)))

    def group(number, carry):
        def load(which):
            return matrix([operands[number, which, plane] for plane in range(18)])

        def store(which, value):
            for plane, part in enumerate(project(value)):
                results[number, which, plane] = part

        here, along, across, side = load(0), load(1), load(2), load(3)
        one = product(here, along)
        two = product(side, across)
        store(0, product(one, dagger(two)))
        store(1, product(across, product(dagger(one), side)))
        store(2, product(along, product(dagger(two), here)))
        return carry

    def round_of(repeat, carry):
        gather_operands()
        lax.fori_loop(0, 3, group, 0)

        zero = jnp.zeros((8, 8, 128), jnp.float32)
        nu_a, nu_b, nu_c = results[0, 2], results[1, 2], results[2, 2]
        mu_a, mu_b, mu_c = results[0, 1], results[1, 1], results[2, 1]
        flip_nu_b = flip(nu_b)
        kicks[0, 0] = select(top, zero, flip(nu_c))
        kicks[0, 1] = select(top, nu_a, flip_nu_b)
        kick_copy(repeat, 0).start()
        kicks[2, 0] = select(top, mu_a, mu_b)
        kicks[2, 1] = select(top, zero, nu_c)
        kicks[1, 0] = select(top, mu_c, zero)
        kicks[1, 1] = select(top, flip_nu_b, nu_a)
        kick_copy(repeat, 1).start()
        kick_copy(repeat, 2).start()

        @pl.when(repeat < 2)
        def _():
            for number, (_, along) in enumerate(EDGES):
                edge_out[number] = select(top, kicks[along, 0], kicks[along, 1])
                edge_copy(repeat, number).start()

        p_a, p_b, p_c = results[0, 0], results[1, 0], results[2, 0]
        q_c = flip(p_c)
        here = (
            p_a + p_b + select(top, p_c, -q_c) + pltpu.roll(select(top, mu_b, mu_a), 1, 2),
            select(top, q_c, -p_c) - p_a - flip(p_b)
            + pltpu.roll(select(top, flip(mu_c), zero), 1, 2),
        )
        factor = jnp.where(repeat == 1, STEP * BETA / 3.0, 0.5 * STEP * BETA / 3.0)
        for half in range(2):
            partial[half] = moment[half] - factor * (
                here[half] + swap_y(select(near_y, kicks[1, half], zero))
            )
        kick_copy(repeat, 0).wait()
        for half in range(2):
            partial[half] -= factor * swap_x(
                select(near_x, kicks[0, half], kicks_in[repeat, 0, half])
            )

        @pl.when(repeat < 2)
        def _():
            for axis in (1, 2):
                moment_copy(repeat, axis).start()

        def arrival(along, value):
            if along == 1:
                return swap_y(select(near_y, zero, value))
            return value

        for along in (2, 1):
            kick_copy(repeat, along).wait()
        for half in range(2):
            moment[half] = partial[half] - factor * (
                arrival(1, kicks_in[repeat, 1, half])
                + kicks_in[repeat, 2, half]
            )

        @pl.when(repeat < 2)
        def _():
            moment_copy(repeat, 0).start()

            def own(half, carry):
                advance(moment.at[half], field.at[half])
                return carry

            lax.fori_loop(0, 2, own, 0)
            for axis in range(3):
                moment_copy(repeat, axis).wait()
                if axis > 0:
                    edge_copy(repeat, axis - 1).wait()
                    edge = edge_in[repeat, axis - 1]
                    edges = (select(top, edge, zero), select(top, zero, edge))
                    for half in range(2):
                        moment_halo[repeat, axis, half] -= factor * (
                            arrival(axis, kicks[axis, half])
                            + arrival(3 - axis, edges[half])
                        )

                def ahead(half, carry):
                    advance(moment_halo.at[repeat, axis, half], halo.at[axis, half])
                    return carry

                lax.fori_loop(0, 2, ahead, 0)

        return carry

    for axis in range(3):
        field_copy(axis).wait()

        for half in range(2):
            for column, (one, two) in enumerate(((1, 2), (2, 0), (0, 1))):
                ar, ai = halo[axis, half, 2 * one], halo[axis, half, 2 * one + 1]
                br, bi = halo[axis, half, 6 + 2 * two], halo[axis, half, 7 + 2 * two]
                cr, ci = halo[axis, half, 2 * two], halo[axis, half, 2 * two + 1]
                dr, di = halo[axis, half, 6 + 2 * one], halo[axis, half, 7 + 2 * one]
                halo[axis, half, 12 + 2 * column] = ar * br - ai * bi - cr * dr + ci * di
                halo[axis, half, 13 + 2 * column] = cr * di + ci * dr - ar * bi - ai * br
    lax.fori_loop(0, 3, round_of, 0)

    for half in range(2):
        for place in range(2):
            rows = slice(4 * place, 4 * place + 4)
            links_out[2 * half + place] = field[half, :, rows, :]
        r01, r02, r12, s01, s02, s12, s00, s11 = [moment[half, plane] for plane in range(8)]
        zero = jnp.zeros_like(r01)
        planes = [
            zero, s00, r01, s01, r02, s02,
            -r01, s01, zero, s11, r12, s12,
            -r02, s02, -r12, s12, zero, -(s00 + s11),
        ]
        for plane, value in enumerate(planes):
            moment_out[2 * half, plane] = value[0:4]
            moment_out[2 * half + 1, plane] = value[4:8]


def body(gauge_links, momenta):
    shape = gauge_links.shape
    assert shape == (4, 3, 3, 2, 2, 2, 1, 128)
    whole = jax.ShapeDtypeStruct((4, 18, 4, 128), jnp.float32)
    vmem = pl.BlockSpec(memory_space=pltpu.VMEM)
    links, moment = pl.pallas_call(
        kernel,
        out_shape=(whole, whole),
        in_specs=[vmem, vmem],
        out_specs=(vmem, vmem),
        scratch_shapes=[
            pltpu.VMEM((2, 18, 8, 128), jnp.float32),
            pltpu.VMEM((3, 2, 18, 8, 128), jnp.float32),
            pltpu.VMEM((2, 8, 8, 128), jnp.float32),
            pltpu.VMEM((2, 8, 8, 128), jnp.float32),
            pltpu.VMEM((2, 3, 2, 8, 8, 128), jnp.float32),
            pltpu.VMEM((3, 2, 8, 8, 128), jnp.float32),
            pltpu.VMEM((3, 3, 2, 8, 8, 128), jnp.float32),
            pltpu.VMEM((2, 8, 8, 128), jnp.float32),
            pltpu.VMEM((2, 2, 8, 8, 128), jnp.float32),
            pltpu.VMEM((3, 4, 18, 8, 128), jnp.float32),
            pltpu.VMEM((3, 3, 8, 8, 128), jnp.float32),
            pltpu.SemaphoreType.DMA((3,)),
            pltpu.SemaphoreType.DMA((3,)),
            pltpu.SemaphoreType.DMA((2, 3)),
            pltpu.SemaphoreType.DMA((2, 3)),
            pltpu.SemaphoreType.DMA((3, 3)),
            pltpu.SemaphoreType.DMA((3, 3)),
            pltpu.SemaphoreType.DMA((2, 2)),
            pltpu.SemaphoreType.DMA((2, 2)),
        ],
        compiler_params=pltpu.CompilerParams(
            collective_id=0, has_side_effects=True, vmem_limit_bytes=16 * 1024 * 1024
        ),
    )(gauge_links.reshape(4, 18, 4, 128), momenta.reshape(4, 18, 4, 128))
    return links.reshape(shape), moment.reshape(shape)


def solution(mesh):
    spec = P(None, None, None, None, "gx", "gy", "gz", None)
    return jax.shard_map(
        body, mesh=mesh, in_specs=(spec, spec), out_specs=(spec, spec), check_vma=False
    )
```

```python
import jax
import jax.numpy as jnp
from jax import lax
from jax.experimental import pallas as pl
from jax.experimental.pallas import tpu as pltpu
from jax.sharding import PartitionSpec as P

BETA = 5.7
STEP = 0.25
AXES = ("gx", "gy", "gz")
MESH = pl.DeviceIdType.MESH
EDGES = ((1, 2), (2, 1))

MOMENT_PLANES = (2, 4, 10, 3, 5, 11, 1, 9)


def matrix(planes):
    return [
        [(planes[(row * 3 + column) * 2], planes[(row * 3 + column) * 2 + 1]) for column in range(3)]
        for row in range(3)
    ]


def dagger(value):
    return ("dagger", value)


def entry(value, row, column):
    if isinstance(value, tuple):
        real, imag = value[1][column][row]
        return real, imag, True
    real, imag = value[row][column]
    return real, imag, False


def product(left, right):
    result = []
    for row in range(3):
        line = []
        for column in range(3):
            real = imag = None
            for inner in range(3):
                lr, li, lc = entry(left, row, inner)
                rr, ri, rc = entry(right, inner, column)
                rr_part = lr * rr
                ii_part = li * ri
                ri_part = lr * ri
                ir_part = li * rr
                first = rr_part - ii_part if lc == rc else rr_part + ii_part
                if real is None:
                    real = first
                    if rc and lc:
                        imag = -(ri_part + ir_part)
                    elif rc:
                        imag = ir_part - ri_part
                    elif lc:
                        imag = ri_part - ir_part
                    else:
                        imag = ri_part + ir_part
                else:
                    real = real + first
                    imag = imag - ri_part if rc else imag + ri_part
                    imag = imag - ir_part if lc else imag + ir_part
            line.append((real, imag))
        result.append(line)
    return result


def project(omega):
    third = (omega[0][0][1] + omega[1][1][1] + omega[2][2][1]) * (1.0 / 3.0)
    return [
        0.5 * (omega[0][1][0] - omega[1][0][0]),
        0.5 * (omega[0][2][0] - omega[2][0][0]),
        0.5 * (omega[1][2][0] - omega[2][1][0]),
        0.5 * (omega[0][1][1] + omega[1][0][1]),
        0.5 * (omega[0][2][1] + omega[2][0][1]),
        0.5 * (omega[1][2][1] + omega[2][1][1]),
        omega[0][0][1] - third,
        omega[1][1][1] - third,
    ]


def exponent(planes):
    r01, r02, r12, s01, s02, s12, s00, s11 = [STEP * plane for plane in planes]
    s22 = -(s00 + s11)
    n01 = s01 * s01 + r01 * r01
    n02 = s02 * s02 + r02 * r02
    n12 = s12 * s12 + r12 * r12
    q00 = s00 * s00 + n01 + n02
    q11 = s11 * s11 + n01 + n12
    q22 = s22 * s22 + n02 + n12
    a_re = s01 * s12 - r01 * r12
    a_im = -(s01 * r12 + r01 * s12)
    q01_re = s02 * s12 + r02 * r12 - s01 * s22
    q01_im = s02 * r12 - r02 * s12 + r01 * s22
    q02_re = a_re - s02 * s11
    q02_im = a_im + r02 * s11
    q12_re = s01 * s02 + r01 * r02 - s12 * s00
    q12_im = r01 * s02 - s01 * r02 + r12 * s00
    half_trace = 0.5 * (q00 + q11 + q22)
    determinant = (
        s00 * (s11 * s22 - n12) - s11 * n02 - s22 * n01 + 2.0 * (a_re * s02 - a_im * r02)
    )
    alpha_im = determinant * (-1.0 / 6.0)
    beta_re = determinant * (1.0 / 24.0)
    beta_im = 1.0 - half_trace * (1.0 / 6.0)
    gamma = half_trace * (1.0 / 24.0) - 0.5

    def diagonal(s, q):
        return 1.0 + beta_re * s + gamma * q, alpha_im + beta_im * s

    def pair(s, r, q_re, q_im):
        even_re = beta_re * s + gamma * q_re
        even_im = gamma * q_im - beta_re * r
        odd_re = beta_im * r
        odd_im = beta_im * s
        upper = (even_re + odd_re, even_im + odd_im)
        lower = (even_re - odd_re, odd_im - even_im)
        return upper, lower

    e01, e10 = pair(s01, r01, q01_re, q01_im)
    e02, e20 = pair(s02, r02, q02_re, q02_im)
    e12, e21 = pair(s12, r12, q12_re, q12_im)
    return [
        [diagonal(s00, q00), e01, e02],
        [e10, diagonal(s11, q11), e12],
        [e20, e21, diagonal(s22, q22)],
    ]


def advance(moment_ref, field_ref):
    step = exponent([moment_ref[plane] for plane in range(8)])
    moved = product(step, matrix([field_ref[plane] for plane in range(18)]))
    for row in range(3):
        for column in range(3):
            for part in range(2):
                field_ref[(row * 3 + column) * 2 + part] = moved[row][column][part]


def kernel(
    links_in, moment_in, links_out, moment_out,
    field, halo, moment, partial, moment_halo, kicks, kicks_in, edge_out, edge_in, field_y, partial_y, kicks_y, operands, results,
    field_send, field_recv, moment_send, moment_recv, kick_send, kick_recv, edge_send, edge_recv,
):
    coords = [lax.axis_index(axis) for axis in AXES]
    counts = [lax.axis_size(axis) for axis in AXES]

    def displaced(*moves):
        place = list(coords)
        for axis, steps in moves:
            place[axis] = lax.rem(coords[axis] + (steps + counts[axis]), counts[axis])
        return tuple(place)

    def neighbour(axis, steps):
        return displaced((axis, steps))

    barrier = pltpu.get_barrier_semaphore()
    for axis in range(3):
        for steps in (-1, 1):
            pl.semaphore_signal(barrier, inc=1, device_id=neighbour(axis, steps), device_id_type=MESH)

    for behind, along in EDGES:
        pl.semaphore_signal(
            barrier, inc=1, device_id=displaced((along, 1), (behind, -1)), device_id_type=MESH
        )

    for half in range(2):
        field[half] = jnp.concatenate([links_in[2 * half], links_in[2 * half + 1]], axis=1)
        for plane, source in enumerate(MOMENT_PLANES):
            moment[half, plane] = jnp.concatenate(
                [moment_in[2 * half, source], moment_in[2 * half + 1, source]], axis=0
            )
    pl.semaphore_wait(barrier, 8)

    def field_copy(axis):
        return pltpu.make_async_remote_copy(
            src_ref=field_y if axis == 1 else field.at[:, pl.ds(0, 12)],
            dst_ref=halo.at[1, 0, pl.ds(0, 12)] if axis == 1 else halo.at[axis, :, pl.ds(0, 12)],
            send_sem=field_send.at[axis], recv_sem=field_recv.at[axis],
            device_id=neighbour(axis, -1), device_id_type=MESH,
        )

    def moment_copy(repeat, axis):
        return pltpu.make_async_remote_copy(
            src_ref=(moment, partial_y, partial)[axis],
            dst_ref=moment_halo.at[repeat, 1, 0] if axis == 1 else moment_halo.at[repeat, axis],
            send_sem=moment_send.at[repeat, axis], recv_sem=moment_recv.at[repeat, axis],
            device_id=neighbour(axis, -1), device_id_type=MESH,
        )

    def kick_copy(repeat, axis):
        return pltpu.make_async_remote_copy(
            src_ref=kicks_y if axis == 1 else kicks.at[axis],
            dst_ref=kicks_in.at[repeat, 1, 0] if axis == 1 else kicks_in.at[repeat, axis],
            send_sem=kick_send.at[repeat, axis], recv_sem=kick_recv.at[repeat, axis],
            device_id=neighbour(axis, 1), device_id_type=MESH,
        )

    def edge_copy(repeat, number):
        behind, along = EDGES[number]
        return pltpu.make_async_remote_copy(
            src_ref=edge_out.at[number], dst_ref=edge_in.at[repeat, number],
            send_sem=edge_send.at[repeat, number], recv_sem=edge_recv.at[repeat, number],
            device_id=displaced((along, 1), (behind, -1)), device_id_type=MESH,
        )

    row = lax.broadcasted_iota(jnp.int32, (1, 8, 128), 1)
    top = row < 4
    near_x = lax.rem(row, 4) < 2
    near_y = lax.rem(row, 2) < 1

    def select(mask, first, second):
        return jnp.where(jnp.broadcast_to(mask, first.shape), first, second)

    def pack_near(first, second):
        return select(near_y, first, pltpu.roll(second, 1, 1))

    def pack_far(first, second):
        return select(near_y, pltpu.roll(second, 7, 1), first)

    field_copy(2).start()
    field_y[...] = pack_near(field[0, 0:12], field[1, 0:12])
    field_copy(1).start()
    field_copy(0).start()

    def flip(value):
        return pltpu.roll(value, 4, 1)

    def swap_x(value):
        return select(near_x, pltpu.roll(value, 6, 1), pltpu.roll(value, 2, 1))

    def swap_y(value):
        return select(near_y, pltpu.roll(value, 7, 1), pltpu.roll(value, 1, 1))

    def ahead_x(half):
        return swap_x(select(near_x, halo[0, half], field[half]))

    def ahead_y(half):
        face = halo[1, 0] if half == 0 else pltpu.roll(halo[1, 0], 7, 1)
        return swap_y(select(near_y, face, field[half]))

    def ahead_t(half):
        return pltpu.roll(field[half], 127, 2)

    def gather_operands():
        operands[0, 0] = field[0]
        operands[1, 0] = field[0]
        operands[0, 3] = field[1]
        operands[1, 3] = flip(field[1])
        operands[2, 0] = select(top, field[0], flip(field[1]))
        operands[2, 3] = select(top, flip(field[0]), field[1])
        x_one = ahead_x(1)
        y_one = ahead_y(1)
        operands[0, 1] = select(top, x_one, y_one)
        operands[1, 1] = flip(select(top, y_one, x_one))
        operands[2, 1] = select(top, flip(ahead_x(0)), halo[2, 1])
        t_zero = ahead_t(0)
        operands[0, 2] = select(top, halo[2, 0], t_zero)
        operands[1, 2] = select(top, t_zero, halo[2, 0])
        operands[2, 2] = select(top, ahead_y(0), flip(ahead_t(1)))

    def group(number, carry):
        def load(which):
            return matrix([operands[number, which, plane] for plane in range(18)])

        def store(which, value):
            for plane, part in enumerate(project(value)):
                results[number, which, plane] = part

        here, along, across, side = load(0), load(1), load(2), load(3)
        one = product(here, along)
        two = product(side, across)
        store(0, product(one, dagger(two)))
        store(1, product(across, product(dagger(one), side)))
        store(2, product(along, product(dagger(two), here)))
        return carry

    def round_of(repeat, carry):
        gather_operands()
        lax.fori_loop(0, 3, group, 0)

        zero = jnp.zeros((8, 8, 128), jnp.float32)
        nu_a, nu_b, nu_c = results[0, 2], results[1, 2], results[2, 2]
        mu_a, mu_b, mu_c = results[0, 1], results[1, 1], results[2, 1]
        flip_nu_b = flip(nu_b)
        kicks[0, 0] = select(top, zero, flip(nu_c))
        kicks[0, 1] = select(top, nu_a, flip_nu_b)
        kick_copy(repeat, 0).start()
        kicks[2, 0] = select(top, mu_a, mu_b)
        kicks[2, 1] = select(top, zero, nu_c)
        kicks[1, 0] = select(top, mu_c, zero)
        kicks[1, 1] = select(top, flip_nu_b, nu_a)
        kicks_y[...] = pack_far(kicks[1, 0], kicks[1, 1])
        kick_copy(repeat, 1).start()
        kick_copy(repeat, 2).start()

        @pl.when(repeat < 2)
        def _():
            for number, (_, along) in enumerate(EDGES):
                edge_out[number] = select(top, kicks[along, 0], kicks[along, 1])
                edge_copy(repeat, number).start()

        p_a, p_b, p_c = results[0, 0], results[1, 0], results[2, 0]
        q_c = flip(p_c)
        here = (
            p_a + p_b + select(top, p_c, -q_c) + pltpu.roll(select(top, mu_b, mu_a), 1, 2),
            select(top, q_c, -p_c) - p_a - flip(p_b)
            + pltpu.roll(select(top, flip(mu_c), zero), 1, 2),
        )
        factor = jnp.where(repeat == 1, STEP * BETA / 3.0, 0.5 * STEP * BETA / 3.0)
        for half in range(2):
            partial[half] = moment[half] - factor * (
                here[half] + swap_y(select(near_y, kicks[1, half], zero))
            )
        kick_copy(repeat, 0).wait()
        for half in range(2):
            partial[half] -= factor * swap_x(
                select(near_x, kicks[0, half], kicks_in[repeat, 0, half])
            )

        @pl.when(repeat < 2)
        def _():
            partial_y[...] = pack_near(partial[0], partial[1])
            for axis in (1, 2):
                moment_copy(repeat, axis).start()

        def arrival(along, value):
            if along == 1:
                return swap_y(select(near_y, zero, value))
            return value

        for along in (2, 1):
            kick_copy(repeat, along).wait()
        for half in range(2):
            moment[half] = partial[half] - factor * (
                arrival(1, kicks_in[repeat, 1, 0] if half == 0 else pltpu.roll(kicks_in[repeat, 1, 0], 1, 1))
                + kicks_in[repeat, 2, half]
            )

        @pl.when(repeat < 2)
        def _():
            moment_copy(repeat, 0).start()

            def own(half, carry):
                advance(moment.at[half], field.at[half])
                return carry

            lax.fori_loop(0, 2, own, 0)
            for axis in range(3):
                moment_copy(repeat, axis).wait()
                if axis > 0:
                    edge_copy(repeat, axis - 1).wait()
                    edge = edge_in[repeat, axis - 1]
                    edges = (select(top, edge, zero), select(top, zero, edge))
                    totals = [
                        arrival(axis, kicks[axis, half]) + arrival(3 - axis, edges[half])
                        for half in range(2)
                    ]
                    if axis == 1:
                        totals = [pack_near(totals[0], totals[1])]
                    for half, total in enumerate(totals):
                        moment_halo[repeat, axis, half] -= factor * total

                def ahead(half, carry):
                    advance(moment_halo.at[repeat, axis, half], halo.at[axis, half])
                    return carry

                lax.fori_loop(0, 1 if axis == 1 else 2, ahead, 0)

        return carry

    for axis in range(3):
        field_copy(axis).wait()

        for half in range(1 if axis == 1 else 2):
            for column, (one, two) in enumerate(((1, 2), (2, 0), (0, 1))):
                ar, ai = halo[axis, half, 2 * one], halo[axis, half, 2 * one + 1]
                br, bi = halo[axis, half, 6 + 2 * two], halo[axis, half, 7 + 2 * two]
                cr, ci = halo[axis, half, 2 * two], halo[axis, half, 2 * two + 1]
                dr, di = halo[axis, half, 6 + 2 * one], halo[axis, half, 7 + 2 * one]
                halo[axis, half, 12 + 2 * column] = ar * br - ai * bi - cr * dr + ci * di
                halo[axis, half, 13 + 2 * column] = cr * di + ci * dr - ar * bi - ai * br
    lax.fori_loop(0, 3, round_of, 0)

    for half in range(2):
        for place in range(2):
            rows = slice(4 * place, 4 * place + 4)
            links_out[2 * half + place] = field[half, :, rows, :]
        r01, r02, r12, s01, s02, s12, s00, s11 = [moment[half, plane] for plane in range(8)]
        zero = jnp.zeros_like(r01)
        planes = [
            zero, s00, r01, s01, r02, s02,
            -r01, s01, zero, s11, r12, s12,
            -r02, s02, -r12, s12, zero, -(s00 + s11),
        ]
        for plane, value in enumerate(planes):
            moment_out[2 * half, plane] = value[0:4]
            moment_out[2 * half + 1, plane] = value[4:8]


def body(gauge_links, momenta):
    shape = gauge_links.shape
    assert shape == (4, 3, 3, 2, 2, 2, 1, 128)
    whole = jax.ShapeDtypeStruct((4, 18, 4, 128), jnp.float32)
    vmem = pl.BlockSpec(memory_space=pltpu.VMEM)
    links, moment = pl.pallas_call(
        kernel,
        out_shape=(whole, whole),
        in_specs=[vmem, vmem],
        out_specs=(vmem, vmem),
        scratch_shapes=[
            pltpu.VMEM((2, 18, 8, 128), jnp.float32),
            pltpu.VMEM((3, 2, 18, 8, 128), jnp.float32),
            pltpu.VMEM((2, 8, 8, 128), jnp.float32),
            pltpu.VMEM((2, 8, 8, 128), jnp.float32),
            pltpu.VMEM((2, 3, 2, 8, 8, 128), jnp.float32),
            pltpu.VMEM((3, 2, 8, 8, 128), jnp.float32),
            pltpu.VMEM((3, 3, 2, 8, 8, 128), jnp.float32),
            pltpu.VMEM((2, 8, 8, 128), jnp.float32),
            pltpu.VMEM((2, 2, 8, 8, 128), jnp.float32),
            pltpu.VMEM((12, 8, 128), jnp.float32),
            pltpu.VMEM((8, 8, 128), jnp.float32),
            pltpu.VMEM((8, 8, 128), jnp.float32),
            pltpu.VMEM((3, 4, 18, 8, 128), jnp.float32),
            pltpu.VMEM((3, 3, 8, 8, 128), jnp.float32),
            pltpu.SemaphoreType.DMA((3,)),
            pltpu.SemaphoreType.DMA((3,)),
            pltpu.SemaphoreType.DMA((2, 3)),
            pltpu.SemaphoreType.DMA((2, 3)),
            pltpu.SemaphoreType.DMA((3, 3)),
            pltpu.SemaphoreType.DMA((3, 3)),
            pltpu.SemaphoreType.DMA((2, 2)),
            pltpu.SemaphoreType.DMA((2, 2)),
        ],
        compiler_params=pltpu.CompilerParams(
            collective_id=0, has_side_effects=True, vmem_limit_bytes=16 * 1024 * 1024
        ),
    )(gauge_links.reshape(4, 18, 4, 128), momenta.reshape(4, 18, 4, 128))
    return links.reshape(shape), moment.reshape(shape)


def solution(mesh):
    spec = P(None, None, None, None, "gx", "gy", "gz", None)
    return jax.shard_map(
        body, mesh=mesh, in_specs=(spec, spec), out_specs=(spec, spec), check_vma=False
    )
```
